32 devices in a mesh: dp: 2 (over core), expert: 4 (over z), tensor: 4 (over y, x).
Axes of the slice: x: 2, y: 2, z: 4, core: 2. Of those that a mesh axis runs over, the one named last changes fastest.
Arguments:
- tokens: bfloat16 [12288, 1024], P(('dp', 'expert', 'tensor')), may hold values from -6 to 6
- segments: int32 [12288], P(('dp', 'expert', 'tensor')), may hold values from 0 to 1535, as said below
- routes: int32 [12288, 8], P(('dp', 'expert', 'tensor')), may hold values from 0 to 31, all different within a row; in each aligned block of 384 rows (0 to 383, 384 to 767, ...) at most 128 rows name the same one
- norm_one: float32 [1024], replicated, may hold values from 0.1 to 1.9
- w_query: bfloat16 [1024, 1024], P(None, 'tensor'), may hold values from -0.1875 to 0.1875
- w_key: bfloat16 [1024, 512], P(None, 'tensor'), may hold values from -0.1875 to 0.1875
- w_value: bfloat16 [1024, 512], P(None, 'tensor'), may hold values from -0.1875 to 0.1875
- w_out: bfloat16 [1024, 1024], P('tensor'), may hold values from -0.5 to 0.5
- norm_two: float32 [1024], replicated, may hold values from 0.1 to 1.9
- w_router: bfloat16 [1024, 32], replicated, may hold values from -0.09375 to 0.09375
- w_gate: bfloat16 [32, 1024, 512], P('expert', None, 'tensor'), may hold values from -0.1875 to 0.1875
- w_up: bfloat16 [32, 1024, 512], P('expert', None, 'tensor'), may hold values from -0.1875 to 0.1875
- w_down: bfloat16 [32, 512, 1024], P('expert', 'tensor'), may hold values from -1 to 1
- cotangent: bfloat16 [12288, 1024], P(('dp', 'expert', 'tensor')), may hold values from -6 to 6
Outputs:
- block_out: bfloat16 [12288, 1024], P(('dp', 'expert', 'tensor'))
- grad_tokens: float32 [12288, 1024], P(('dp', 'expert', 'tensor'))
- grad_norm_one: float32 [1024], replicated
- grad_query: float32 [1024, 1024], P(None, 'tensor')
- grad_key: float32 [1024, 512], P(None, 'tensor')
- grad_value: float32 [1024, 512], P(None, 'tensor')
- grad_out: float32 [1024, 1024], P('tensor')
- grad_norm_two: float32 [1024], replicated
- grad_router: float32 [1024, 32], replicated
- grad_gate: float32 [32, 1024, 512], P('expert', None, 'tensor')
- grad_up: float32 [32, 1024, 512], P('expert', None, 'tensor')
- grad_down: float32 [32, 512, 1024], P('expert', 'tensor')
The draws below stay inside these ranges and needn't reach their ends.
Inputs may be any that keep to these rules, and one draw needn't show every extreme that they name: `segments`: within each sequence of 1536 tokens the segment numbers start at 0 and never fall; the last segment of every sequence is numbered 1536 - 1; in every sequence one segment begins among its first 384 tokens and ends among its last 384. `routes`: each row names 8 different experts. Among the rows of one device no expert is named by more than 128 rows, a bound that some block reaches.
All inputs are finite; a program needn't handle non-finite values.
Results may differ from the reference program's by a relative error of at most 0.023.
Values may be sent and summed in bfloat16 or wider, within the bound.
A program may use at most 256 MiB of HBM per device.

```python
import math
import jax
import jax.numpy as jnp
import numpy as np
from jax import lax

D = 1024
HEADS = 16
KV_HEADS = 8
HEAD = 64
FF = 512
EXPERTS = 32
TOP = 8
TOK_DEV = 384
SEQ_LEN = 1536
TOKENS = 12288
CAP = 128


def draw_segments(key, part):
    key = jax.random.fold_in(key, 11)
    groups = TOKENS // SEQ_LEN
    key_list = jax.random.split(key, 3)
    doc_start = jax.random.randint(key_list[0], (groups, 1), 1, TOK_DEV)
    doc_stop = SEQ_LEN - jax.random.randint(key_list[1], (groups, 1), 1, TOK_DEV)
    places = jnp.arange(SEQ_LEN, dtype=jnp.int32)[None, :]
    coins = jax.random.randint(key_list[2], (groups, SEQ_LEN), 0, 24)
    outside = (places < doc_start) | (places >= doc_stop)
    breaks = (coins == 0) & outside | (places == doc_start) | (places == doc_stop)
    breaks = breaks & (places > 0)
    counted = jnp.cumsum(breaks.astype(jnp.int32), axis=1).astype(jnp.int32)
    final_count = counted[:, -1:]
    numbered = jnp.where(counted == final_count, SEQ_LEN - 1, counted)
    return numbered.reshape(TOKENS).astype(jnp.int32)


def levels(key, extent, cuts, smallest, high):
    def one(dim, blocks):
        heights = jax.random.uniform(jax.random.fold_in(jax.random.fold_in(key, 6), dim), (blocks,), jnp.float32, smallest / len(cuts), high / len(cuts))
        return jnp.repeat(jnp.exp(heights), extent[dim] // blocks).reshape((-1,) + (1,) * (len(extent) - dim - 1))

    loudness = one(*cuts[0])
    for cut in cuts[1:]:
        loudness = loudness * one(*cut)
    return loudness


def routed_block(stream_key, own, number, rows, number_of, top, limit, skew):
    order = jax.random.permutation(stream_key, number_of)
    packed, common = portions_of(number_of, rows * top, limit, skew, True), portions_of(number_of, rows * top, limit, skew, False)
    places = jnp.arange(number_of)

    def named(tallies, turn):
        used = int((tallies > 0).sum())
        fixed = max(1, used // 4)
        moved = fixed + (places - fixed + turn * (used - fixed)) % max(1, number_of - fixed)
        return jnp.zeros((number_of,), jnp.int32).at[order[jnp.where(places < fixed, places, moved)]].set(jnp.asarray(tallies, jnp.int32))

    tallies = jnp.where(number % 4 == 0, named(packed, number // 4), named(common, number - number // 4 - 1))
    mixed = jax.random.permutation(jax.random.fold_in(own, 3), number_of)
    source_of, taker = mixed[0:number_of // 2 * 2:2], mixed[1:number_of // 2 * 2:2]
    margin = jnp.minimum(tallies[source_of] - 1, limit - tallies[taker]) // 2
    margin = jnp.where((source_of == order[0]) | (taker == order[0]) | (tallies[taker] == 0), 0, jnp.maximum(margin, 0))
    moved = jax.random.randint(jax.random.fold_in(own, 4), (number_of // 2,), 0, 1 << 20) % (margin + 1)
    tallies = tallies.at[source_of].add(-moved).at[taker].add(moved)
    members = jnp.searchsorted(jnp.cumsum(tallies), jnp.arange(rows * top), side="right").astype(jnp.int32)
    listing = members.reshape(top, rows).T
    listing = listing[jax.random.permutation(jax.random.fold_in(own, 1), rows)]
    turn = jax.random.randint(jax.random.fold_in(own, 2), (rows, 1), 0, top)
    return jnp.take_along_axis(listing, (jnp.arange(top)[None, :] + turn) % top, axis=1)


def portions_of(amount, total, limit, lean, full):
    portions = [(1 << 20) // math.isqrt(grade ** lean) + 1 for grade in range(1, amount + 1)]
    largest = limit if full else min(limit, max(-(-total // amount), total * portions[0] // sum(portions)))
    least = 1 if total - largest >= amount - 1 else 0
    counts, surplus = [largest] + [least] * (amount - 1), total - largest - least * (amount - 1)
    while surplus > 0:
        free = [i for i in range(1, amount) if counts[i] < largest] or [i for i in range(1, amount) if counts[i] < limit]
        pool, left = sum([portions[i] for i in free]), surplus
        for i in free:
            more = min(limit - counts[i], max(1, left * portions[i] // pool), surplus)
            counts[i] = counts[i] + more
            surplus = surplus - more
    return np.array(counts)


def scatter_about(own_key, dims, width, limit, cuts=(), held_as=jnp.bfloat16):
    array = width * jax.random.normal(own_key, dims, jnp.float32)
    if cuts:
        array = array * levels(own_key, dims, cuts, -0.22, 0.18)
    return jnp.clip(array, -limit, limit).astype(held_as)


def setup_inputs(seed: int = 0) -> dict:
    arg_keys = jax.random.split(jax.random.key(seed), 15)
    tokens = scatter_about(arg_keys[0], (TOKENS, D), 1.0, 6.0, ((0, 32),))
    segments = draw_segments(jax.random.fold_in(arg_keys[14], 71), 0)
    routes_keys = jax.random.split(jax.random.fold_in(arg_keys[2], 1), TOKENS // TOK_DEV)
    routes_turns = jax.random.permutation(jax.random.fold_in(arg_keys[2], 3), TOKENS // TOK_DEV)
    routes = jax.vmap(lambda own, number: routed_block(jax.random.fold_in(arg_keys[2], 2), own, number, TOK_DEV, EXPERTS, TOP, CAP, 1))(routes_keys, routes_turns).reshape((TOKENS, TOP))
    norm_one = jnp.clip(1.0 + 0.18 * jax.random.normal(arg_keys[3], (D,), jnp.float32), 0.1, 1.9)
    w_query = scatter_about(arg_keys[4], (D, HEADS * HEAD), D ** -0.5, 0.1875, ((1, 4),))
    w_key = scatter_about(arg_keys[5], (D, KV_HEADS * HEAD), D ** -0.5, 0.1875, ((1, 4),))
    w_value = scatter_about(arg_keys[6], (D, KV_HEADS * HEAD), D ** -0.5, 0.1875, ((1, 4),))
    w_out = scatter_about(arg_keys[7], (HEADS * HEAD, D), (HEADS * HEAD // 8) ** -0.5, 0.5, ((0, 4),))
    norm_two = jnp.clip(1.0 + 0.18 * jax.random.normal(arg_keys[8], (D,), jnp.float32), 0.1, 1.9)
    w_router = scatter_about(arg_keys[9], (D, EXPERTS), (0.5 * D ** -0.5), 0.09375)
    w_gate = scatter_about(arg_keys[10], (EXPERTS, D, FF), D ** -0.5, 0.1875, ((0, 4), (2, 4)))
    w_up = scatter_about(arg_keys[11], (EXPERTS, D, FF), D ** -0.5, 0.1875, ((0, 4), (2, 4)))
    w_down = scatter_about(arg_keys[12], (EXPERTS, FF, D), (FF // 16) ** -0.5, 1.0, ((0, 4), (1, 4)))
    cotangent = scatter_about(arg_keys[13], (TOKENS, D), 1.0, 6.0, ((0, 32),))
    return dict(tokens=tokens, segments=segments, routes=routes, norm_one=norm_one, w_query=w_query, w_key=w_key, w_value=w_value, w_out=w_out, norm_two=norm_two, w_router=w_router, w_gate=w_gate, w_up=w_up, w_down=w_down, cotangent=cotangent)


@jax.custom_vjp
def low(v):
    return lax.optimization_barrier(v.astype(jnp.bfloat16)).astype(jnp.float32)

@jax.custom_vjp
def low_back(v):
    return v

def low_keep(v):
    return (low(v), None)

def low_pass(kept, grad):
    return (grad,)

def back_keep(v):
    return (v, None)

def back_low(kept, grad):
    return (low(grad),)
low.defvjp(low_keep, low_pass)
low_back.defvjp(back_keep, back_low)
epsilon = 1e-06
highest = lax.Precision.HIGHEST

def rms_norm(features, gain_vec):
    return features * lax.rsqrt(lax.optimization_barrier(jnp.mean(features * features, axis=-1, keepdims=True)) + epsilon) * gain_vec

def rotate(vectors, places):
    half_dim = vectors.shape[-1] // 2
    frequency = 10000.0 ** (-jnp.arange(half_dim, dtype=jnp.float32) / half_dim)
    angles = places.astype(jnp.float32)[:, None] * frequency[None, :]
    cosine = jnp.cos(angles)[:, None, :]
    sine_part = jnp.sin(angles)[:, None, :]
    front_half = vectors[..., :half_dim]
    back_half = vectors[..., half_dim:]
    return jnp.concatenate([front_half * cosine - back_half * sine_part, back_half * cosine + front_half * sine_part], axis=-1)

def slot_ranks(routes):
    route_rows = routes.reshape(-1, TOK_DEV * TOP)
    expert_marks = (route_rows[:, :, None] == jnp.arange(EXPERTS, dtype=jnp.int32)[None, None, :]).astype(jnp.int32)
    earlier = jnp.cumsum(expert_marks, axis=1) - expert_marks
    return lax.optimization_barrier(jnp.sum(earlier * expert_marks, axis=2)).reshape(-1).astype(jnp.int32)

def attend_group(queries, key_rows, value_rows, seg_rows):
    block_count = max(1, SEQ_LEN // 512)
    block_rows = SEQ_LEN // block_count
    places = jnp.arange(SEQ_LEN, dtype=jnp.int32)
    score_scale = HEAD ** (-0.5)

    def one_block(pieces):
        query_block, query_places, query_segs = pieces
        raw_scores = jnp.einsum('qkgd,skd->kgqs', query_block, key_rows, precision=highest) * score_scale
        scores = low_back(raw_scores)
        allowed = (places[None, :] <= query_places[:, None]) & (seg_rows[None, :] == query_segs[:, None])
        masked = jnp.where(allowed, scores, -1e+30)
        largest = lax.optimization_barrier(jnp.max(masked, axis=-1, keepdims=True))
        weights = jnp.exp(masked - largest)
        prob_rows = low(weights / lax.optimization_barrier(jnp.sum(weights, axis=-1, keepdims=True)))
        return jnp.einsum('kgqs,skd->qkgd', prob_rows, value_rows, precision=highest)
    pieces = (queries.reshape((block_count, block_rows) + queries.shape[1:]), places.reshape(block_count, block_rows), seg_rows.reshape(block_count, block_rows))
    return lax.map(jax.checkpoint(one_block), pieces).reshape(queries.shape)

def forward(tokens, norm_one, w_query, w_key, w_value, w_out, norm_two, w_router, w_gate, w_up, w_down, segments, routes, sources):
    groups = TOKENS // SEQ_LEN
    group_size = HEADS // KV_HEADS
    places = jnp.arange(TOKENS, dtype=jnp.int32) % SEQ_LEN
    normed = low(rms_norm(tokens, norm_one))
    query_raw = low_back(jnp.dot(normed, w_query, precision=highest))
    key_raw = low_back(jnp.dot(normed, w_key, precision=highest))
    queries = low(rotate(query_raw.reshape(TOKENS, HEADS, HEAD), places))
    key_rows = low(rotate(key_raw.reshape(TOKENS, KV_HEADS, HEAD), places))
    value_rows = low_back(low(jnp.dot(normed, w_value, precision=highest)))
    grouped = (queries.reshape(groups, SEQ_LEN, KV_HEADS, group_size, HEAD), key_rows.reshape(groups, SEQ_LEN, KV_HEADS, HEAD), value_rows.reshape(groups, SEQ_LEN, KV_HEADS, HEAD), segments.reshape(groups, SEQ_LEN))

    def step_group(carry_value, pieces):
        return (carry_value, attend_group(pieces[0], pieces[1], pieces[2], pieces[3]))
    carry_value, mixed_heads = lax.scan(step_group, jnp.zeros((), jnp.float32), grouped)
    mixed_heads = low_back(low(mixed_heads.reshape(TOKENS, HEADS * HEAD)))
    attention = low_back(jnp.dot(mixed_heads, w_out, precision=highest))
    hidden = tokens + attention
    routed = low(rms_norm(hidden, norm_two))
    logits = jnp.dot(routed, w_router, precision=highest)
    chosen = jnp.take_along_axis(logits, routes, axis=1)
    gate_probs = jax.nn.softmax(chosen, axis=-1)
    routed_pad = jnp.concatenate([routed, jnp.zeros((1, D), routed.dtype)], axis=0)
    gates_pad = jnp.concatenate([gate_probs.reshape(-1), jnp.zeros((1,), gate_probs.dtype)], axis=0)

    def one_expert(pieces):
        source_row, gate_matrix, up_matrix, down_matrix = pieces
        expert_rows = low_back(routed_pad[source_row // TOP])
        gate_val = low_back(jnp.dot(expert_rows, gate_matrix, precision=highest))
        up_val = low_back(jnp.dot(expert_rows, up_matrix, precision=highest))
        inner_rows = low(jax.nn.silu(gate_val) * up_val)
        expert_out = low_back(low(jnp.dot(inner_rows, down_matrix, precision=highest)))
        return gates_pad[source_row][:, None] * expert_out
    contributions = lax.map(jax.checkpoint(one_expert), (sources, w_gate, w_up, w_down))
    mixture = jnp.zeros((TOKENS + 1, D), hidden.dtype).at[(sources // TOP).reshape(-1)].add(contributions.reshape(-1, D))
    return hidden + mixture[:TOKENS]

def reference(tokens, segments, routes, norm_one, w_query, w_key, w_value, w_out, norm_two, w_router, w_gate, w_up, w_down, cotangent):
    blocks = TOKENS // TOK_DEV
    entry_ids = jnp.arange(TOKENS * TOP, dtype=jnp.int32)
    block_ids = (entry_ids // (TOK_DEV * TOP)).astype(jnp.int32)
    route_flat = routes.reshape(-1).astype(jnp.int32)
    position = (block_ids * CAP + slot_ranks(routes)).astype(jnp.int32)
    sources = jnp.full((EXPERTS, blocks * CAP), TOKENS * TOP, jnp.int32).at[route_flat, position].set(entry_ids)
    floats = (tokens.astype(jnp.float32), norm_one, w_query.astype(jnp.float32), w_key.astype(jnp.float32), w_value.astype(jnp.float32), w_out.astype(jnp.float32), norm_two, w_router.astype(jnp.float32), w_gate.astype(jnp.float32), w_up.astype(jnp.float32), w_down.astype(jnp.float32))

    def whole_layer(*params):
        return forward(*params, segments, routes, sources)
    output, pullback = jax.vjp(whole_layer, *floats)
    gradients = pullback(cotangent.astype(jnp.float32))
    return (output.astype(jnp.bfloat16), gradients[0], gradients[1], gradients[2], gradients[3], gradients[4], gradients[5], gradients[6], gradients[7], gradients[8], gradients[9], gradients[10])
```

```python
import jax
import jax.numpy as jnp
from jax import lax
from jax.sharding import PartitionSpec as P

HEAD = 64
CAP = 128


epsilon = 1e-06
highest = lax.Precision.HIGHEST


def rms_norm(features, gain_vec):
    return (
        features
        * lax.rsqrt(jnp.mean(features * features, axis=-1, keepdims=True) + epsilon)
        * gain_vec
    )


def rotate(vectors, places):
    half_dim = vectors.shape[-1] // 2
    frequency = 10000.0 ** (-jnp.arange(half_dim, dtype=jnp.float32) / half_dim)
    angles = places.astype(jnp.float32)[:, None] * frequency[None, :]
    cosine = jnp.cos(angles)[:, None, :]
    sine_part = jnp.sin(angles)[:, None, :]
    front_half = vectors[..., :half_dim]
    back_half = vectors[..., half_dim:]
    return jnp.concatenate(
        [front_half * cosine - back_half * sine_part, back_half * cosine + front_half * sine_part],
        axis=-1,
    )


def contract_rows(left_in, right_in):
    return lax.dot_general(
        left_in, right_in, (((0,), (0,)), ((), ())), preferred_element_type=jnp.float32
    )


def contract_cols(left_in, right_in):
    return lax.dot_general(
        left_in, right_in, (((1,), (1,)), ((), ())), preferred_element_type=jnp.float32
    )


def gather_over(array, axis_name, dim=0):
    return lax.all_gather(array, axis_name, axis=dim, tiled=True)


def scatter_over(array, axis_name, dim=0):
    return lax.psum_scatter(array, axis_name, scatter_dimension=dim, tiled=True)


def swap_cores(array):
    return lax.ppermute(array, "dp", [(0, 1), (1, 0)])


def own_half(weight):
    half = weight.shape[1] // 2
    return lax.dynamic_slice_in_dim(weight, lax.axis_index("dp") * half, half, axis=1)


def join_halves(mine, theirs):
    first = lax.axis_index("dp") == 0
    return jnp.concatenate(
        [jnp.where(first, mine, theirs), jnp.where(first, theirs, mine)], axis=1
    )


def body(
    tokens,
    segments,
    routes,
    norm_one,
    w_query,
    w_key,
    w_value,
    w_out,
    norm_two,
    w_router,
    w_gate,
    w_up,
    w_down,
    cotangent,
):
    f32, bf16 = jnp.float32, jnp.bfloat16
    local_rows, model_width = tokens.shape
    query_cols, kv_cols = w_query.shape[1], w_key.shape[1]
    head_local, kv_local = query_cols // HEAD, kv_cols // HEAD
    group_size = head_local // kv_local
    expert_local = w_gate.shape[0]
    owner_count = lax.axis_size("expert")
    experts_all = expert_local * owner_count
    score_scale = HEAD ** (-0.5)
    first_expert = lax.axis_index("expert") * expert_local

    inputs = tokens.astype(f32)
    normed_one, norm_back_one = jax.vjp(rms_norm, inputs, norm_one)
    normed = normed_one.astype(bf16)
    normed_all = gather_over(normed, "tensor")
    segs_all = gather_over(segments, "tensor")

    gate_mine = gather_over(own_half(jnp.swapaxes(w_gate, 1, 2)), "tensor", 1)
    up_mine = gather_over(own_half(jnp.swapaxes(w_up, 1, 2)), "tensor", 1)
    down_mine = gather_over(own_half(w_down), "tensor", 1)
    half_units = gate_mine.shape[1]
    units = 2 * half_units
    gate_up = jnp.concatenate(
        [gate_mine, swap_cores(gate_mine), up_mine, swap_cores(up_mine)], axis=1
    )
    down = jnp.concatenate([down_mine, swap_cores(down_mine)], axis=1)

    routes_all = lax.all_gather(routes, "expert", axis=0)
    local_ids = first_expert + jnp.arange(expert_local, dtype=jnp.int32)
    marks = jnp.any(routes_all[:, None, :, :] == local_ids[None, :, None, None], axis=-1)
    order = jnp.arange(local_rows, dtype=jnp.int32)
    earlier = (order[:, None] < order[None, :]).astype(bf16)
    ranks = jnp.einsum("nlt,tu->nlu", marks.astype(bf16), earlier, preferred_element_type=f32)
    places_of = jnp.where(marks, ranks.astype(jnp.int32), -1)
    in_slot = places_of[:, :, None, :] == jnp.arange(CAP, dtype=jnp.int32)[None, None, :, None]
    pick = in_slot.astype(bf16)

    def to_slots(rows_all):
        return jnp.einsum("nlct,ntd->nlcd", pick, rows_all, preferred_element_type=f32).astype(bf16)

    def to_rows(slots):
        return jnp.einsum("nlct,nlcd->ntd", pick, slots, preferred_element_type=f32).astype(bf16)

    up_slots = to_slots(lax.all_gather(cotangent, "expert", axis=0))

    length = normed_all.shape[0]
    places = jnp.arange(length, dtype=jnp.int32)
    w_qkv = jnp.concatenate([w_query, w_key, w_value], axis=1)
    qkv = jnp.dot(normed_all, w_qkv, preferred_element_type=f32)
    query_raw = qkv[:, :query_cols].reshape(length, head_local, HEAD)
    key_raw = qkv[:, query_cols : query_cols + kv_cols].reshape(length, kv_local, HEAD)
    value_rows = qkv[:, query_cols + kv_cols :].astype(bf16).reshape(length, kv_local, HEAD)
    query_turned, rope_query = jax.vjp(lambda vectors: rotate(vectors, places), query_raw)
    key_turned, rope_key = jax.vjp(lambda vectors: rotate(vectors, places), key_raw)
    key_rows = key_turned.astype(bf16)
    queries = query_turned.astype(bf16).reshape(length, kv_local, group_size, HEAD)
    block_count = max(1, length // 512)
    block_rows = length // block_count

    def block_scores(block):
        start, end = block * block_rows, (block + 1) * block_rows
        scores = (
            jnp.einsum(
                "qkgd,skd->kgqs", queries[start:end], key_rows[:end], preferred_element_type=f32
            )
            * score_scale
        )
        allowed = (places[None, :end] <= places[start:end, None]) & (
            segs_all[None, :end] == segs_all[start:end, None]
        )
        return jnp.where(allowed, scores, -1e30)

    mixed_parts, log_totals = [], []
    for block in range(block_count):
        end = (block + 1) * block_rows
        masked = block_scores(block)
        largest = jnp.max(masked, axis=-1, keepdims=True)
        weights = jnp.exp(masked - largest)
        row_total = jnp.sum(weights, axis=-1, keepdims=True)
        prob_rows = (weights / row_total).astype(bf16)
        mixed_parts.append(
            jnp.einsum("kgqs,skd->qkgd", prob_rows, value_rows[:end], preferred_element_type=f32)
            .astype(bf16)
            .reshape(block_rows, query_cols)
        )
        log_totals.append(largest + jnp.log(row_total))
    mixed_heads = jnp.concatenate(mixed_parts, axis=0)
    attention = scatter_over(
        jnp.dot(mixed_heads, w_out, preferred_element_type=f32).astype(bf16), "tensor"
    ).astype(f32)
    hidden = inputs + attention
    normed_two, norm_back_two = jax.vjp(rms_norm, hidden, norm_two)
    routed = normed_two.astype(bf16)
    row_slots = to_slots(lax.all_gather(routed, "expert", axis=0))

    logits = jnp.dot(routed, w_router, preferred_element_type=f32)
    route_onehot = (
        routes[:, :, None] == jnp.arange(experts_all, dtype=jnp.int32)[None, None, :]
    ).astype(f32)
    chosen = jnp.sum(route_onehot * logits[:, None, :], axis=-1)
    gate_probs = jax.nn.softmax(chosen, axis=-1)
    gate_table = jnp.sum(route_onehot * gate_probs[:, :, None], axis=1)
    gates_all = lax.all_to_all(
        gate_table.T.reshape(owner_count, expert_local, local_rows), "expert", 0, 0, tiled=True
    )
    gate_slots = jnp.sum(jnp.where(in_slot, gates_all[:, :, None, :], 0.0), axis=-1)[..., None]

    both_val = jnp.einsum("nlcd,lfd->nlcf", row_slots, gate_up, preferred_element_type=f32)
    gate_val, up_val = both_val[..., :units], both_val[..., units:]
    sigmoid = jax.nn.sigmoid(gate_val)
    silu = gate_val * sigmoid
    inner = silu * up_val
    gated_inner = (gate_slots * inner).astype(bf16)
    down_back = jnp.einsum("nlcd,lfd->nlcf", up_slots, down, preferred_element_type=f32)
    gate_grad_slots = jnp.sum(inner * down_back, axis=-1)
    inner_grad = gate_slots * down_back
    both_back = jnp.concatenate(
        [
            (inner_grad * up_val * (sigmoid * (1.0 + gate_val * (1.0 - sigmoid)))).astype(bf16),
            (inner_grad * silu).astype(bf16),
        ],
        axis=-1,
    )
    row_back = to_rows(
        jnp.einsum("nlcf,lfd->nlcd", both_back, gate_up, preferred_element_type=f32).astype(bf16)
    )
    routed_grad = scatter_over(
        row_back.reshape(owner_count * local_rows, model_width), "expert"
    ).astype(f32)
    gate_grads = lax.all_to_all(
        jnp.sum(jnp.where(in_slot, gate_grad_slots[..., None], 0.0), axis=2),
        "expert",
        0,
        0,
        tiled=True,
    ).reshape(experts_all, local_rows)
    gate_grad = jnp.sum(route_onehot * gate_grads.T[:, None, :], axis=-1)
    expert_rows = to_rows(
        jnp.einsum("nlcf,lfd->nlcd", gated_inner, down, preferred_element_type=f32).astype(bf16)
    )
    block_out = hidden + scatter_over(
        expert_rows.reshape(owner_count * local_rows, model_width), "expert"
    ).astype(f32)

    both_wgrad = jnp.einsum("nlcf,nlcd->lfd", both_back, row_slots, preferred_element_type=f32)
    down_wgrad = jnp.einsum("nlcf,nlcd->lfd", gated_inner, up_slots, preferred_element_type=f32)

    def reduced(wgrad, start):
        theirs = wgrad[:, start + half_units : start + units].astype(bf16)
        total = wgrad[:, start : start + half_units].astype(bf16) + swap_cores(theirs)
        part = scatter_over(total, "tensor", 1)
        return join_halves(part, swap_cores(part)).astype(f32)

    gate_out = jnp.swapaxes(reduced(both_wgrad, 0), 1, 2)
    up_out = jnp.swapaxes(reduced(both_wgrad, units), 1, 2)
    down_out = reduced(down_wgrad, 0)

    upstream = cotangent.astype(f32)
    chosen_grad = gate_probs * (gate_grad - jnp.sum(gate_probs * gate_grad, axis=-1, keepdims=True))
    logit_grad = jnp.sum(route_onehot * chosen_grad[:, :, None], axis=1)
    routed_grad = routed_grad + lax.dot_general(
        logit_grad, w_router.astype(f32), (((1,), (1,)), ((), ())), precision=highest
    )
    router_grad = lax.dot_general(
        routed.astype(f32), logit_grad, (((0,), (0,)), ((), ())), precision=highest
    )
    hidden_part, norm_two_grad = norm_back_two(routed_grad)
    hidden_grad = upstream + hidden_part
    attn_all = gather_over(hidden_grad.astype(bf16), "tensor")
    router_grad, norm_two_grad = lax.psum(
        (router_grad, norm_two_grad), ("dp", "expert", "tensor")
    )
    out_wgrad = lax.psum(contract_rows(mixed_heads, attn_all).astype(bf16), ("dp", "expert"))
    mixed_grad = (
        contract_cols(attn_all, w_out).astype(bf16).reshape(length, kv_local, group_size, HEAD)
    )
    key_parts = [0.0] * block_count
    value_parts = [0.0] * block_count
    query_parts = []
    for block in range(block_count):
        start, end = block * block_rows, (block + 1) * block_rows
        grad_block = mixed_grad[start:end]
        prob_full = jnp.exp(block_scores(block) - log_totals[block])
        prob_grad = jnp.einsum(
            "qkgd,skd->kgqs", grad_block, value_rows[:end], preferred_element_type=f32
        )
        value_grad = jnp.einsum(
            "kgqs,qkgd->skd", prob_full.astype(bf16), grad_block, preferred_element_type=f32
        )
        centred = jnp.sum(prob_full * prob_grad, axis=-1, keepdims=True)
        score_grad = (prob_full * (prob_grad - centred)).astype(bf16)
        query_parts.append(
            jnp.einsum("kgqs,skd->qkgd", score_grad, key_rows[:end], preferred_element_type=f32)
            * score_scale
        )
        key_grad = (
            jnp.einsum("kgqs,qkgd->skd", score_grad, queries[start:end], preferred_element_type=f32)
            * score_scale
        )
        for part in range(block + 1):
            rows = slice(part * block_rows, (part + 1) * block_rows)
            key_parts[part] = key_parts[part] + key_grad[rows]
            value_parts[part] = value_parts[part] + value_grad[rows]
    (query_raw_grad,) = rope_query(
        jnp.concatenate(query_parts, axis=0).reshape(length, head_local, HEAD)
    )
    (key_raw_grad,) = rope_key(jnp.concatenate(key_parts, axis=0))
    qkv_low = jnp.concatenate(
        [
            query_raw_grad.reshape(length, query_cols).astype(bf16),
            key_raw_grad.reshape(length, kv_cols).astype(bf16),
            jnp.concatenate(value_parts, axis=0).reshape(length, kv_cols).astype(bf16),
        ],
        axis=1,
    )
    normed_grad = scatter_over(contract_cols(qkv_low, w_qkv).astype(bf16), "tensor").astype(f32)
    qkv_wgrad = lax.psum(
        contract_rows(normed_all, qkv_low).astype(bf16), ("dp", "expert")
    ).astype(f32)
    input_part, norm_one_grad = norm_back_one(normed_grad)
    norm_one_grad = lax.psum(norm_one_grad, ("dp", "expert", "tensor"))
    return (
        block_out.astype(bf16),
        hidden_grad + input_part,
        norm_one_grad,
        qkv_wgrad[:, :query_cols],
        qkv_wgrad[:, query_cols : query_cols + kv_cols],
        qkv_wgrad[:, query_cols + kv_cols :],
        out_wgrad.astype(f32),
        norm_two_grad,
        router_grad,
        gate_out,
        up_out,
        down_out,
    )


def solution(mesh):
    placed = (
        P(("dp", "expert", "tensor"), None),
        P(("dp", "expert", "tensor")),
        P(("dp", "expert", "tensor"), None),
        P(),
        P(None, "tensor"),
        P(None, "tensor"),
        P(None, "tensor"),
        P("tensor", None),
        P(),
        P(),
        P("expert", None, "tensor"),
        P("expert", None, "tensor"),
        P("expert", "tensor", None),
        P(("dp", "expert", "tensor"), None),
    )
    return jax.shard_map(
        body,
        mesh=mesh,
        in_specs=placed,
        out_specs=(
            P(("dp", "expert", "tensor"), None),
            P(("dp", "expert", "tensor"), None),
            P(),
            P(None, "tensor"),
            P(None, "tensor"),
            P(None, "tensor"),
            P("tensor", None),
            P(),
            P(),
            P("expert", None, "tensor"),
            P("expert", None, "tensor"),
            P("expert", "tensor", None),
        ),
        check_vma=False,
    )
```
